768 devices in a mesh: tab: 8 (over x, core), rep: 96 (over z, y).
Axes of the slice: x: 4, y: 8, z: 12, core: 2. Of those that a mesh axis runs over, the one named last changes fastest.
Arguments:
- d_proj: bfloat16 [96, 1024, 8, 256], P('rep', 'tab'), may hold values from -6 to 6
- pooled: bfloat16 [96, 1024, 8, 512], P('rep', 'tab'), may hold values from -6 to 6
- proj: bfloat16 [8, 512, 256], replicated, may hold values from -0.25 to 0.25
- bag_rows: int32 [96, 1024, 8, 8], P('rep', None, 'tab'), may hold values from 0 to 511
- bag_lengths: int32 [96, 1024, 8], P('rep', None, 'tab'), may hold values from 1 to 8
- dim_blocks: int32 [8], replicated, may hold values from 1 to 16
Outputs:
- emb_grad: float32 [8, 512, 512], P('tab')
- proj_grad: float32 [8, 512, 256], P('tab')
The draws below stay inside these ranges and needn't reach their ends.
All inputs are finite; a program needn't handle non-finite values.
Results may differ from the reference program's by a relative error of at most 0.003.
Values may be sent and summed in bfloat16 or wider, within the bound.
No kernel may reach another device: no remote copies, remote signals or barrier semaphores. Data moves between devices by JAX's collectives and lax.ppermute only.
A program may use at most 32 MiB of HBM per device.

```python
import math
import jax
import jax.numpy as jnp
import numpy as np
from jax import lax

ROWS = 512
BAG = 8
EMAX = 512
P_SIZE = 256
UNIT = 32
TABLES = 8
GROUPS = 96
GROUP_B = 1024


def plant(values, key, least, high):
    index_at = [jax.random.randint(jax.random.fold_in(key, axis), (), 0, length) for axis, length in enumerate(values.shape)]
    longest = values.shape.index(max(values.shape))
    neighbour = index_at[:longest] + [(index_at[longest] + 1) % values.shape[longest]] + index_at[longest + 1:]
    return values.at[tuple(index_at)].set(least).at[tuple(neighbour)].set(high)


def block_scale(rng, extent, shards, smallest, top_value):
    factor_of = 1.0
    for position, blocks in shards:
        steps = jax.random.uniform(jax.random.fold_in(jax.random.fold_in(rng, 6), position), (blocks,), jnp.float32, smallest / len(shards), top_value / len(shards))
        factor_of = factor_of * jnp.repeat(jnp.exp(steps), extent[position] // blocks).reshape((-1,) + (1,) * (len(extent) - 1 - position))
    return factor_of


def cumulative_ranks(number_of, skew):
    loads = [(1 << 20) // math.isqrt(standing ** skew) + 1 for standing in range(1, number_of + 1)]
    scale = 1 + sum(loads) // (1 << 30)
    return np.cumsum(np.array([max(1, weight // scale) for weight in loads]))


def ranked(rng, dims, count, skew):
    grid = cumulative_ranks(count, skew)
    pick = jax.random.randint(jax.random.fold_in(rng, 1), dims, 0, int(grid[count - 1]))
    grade = jnp.searchsorted(jnp.asarray(grid, jnp.int32), pick, side="right")
    return jax.random.permutation(jax.random.fold_in(rng, 2), count)[grade].astype(jnp.int32)


def centred(stream_key, dims, scale, reach, shards=(), kind=jnp.bfloat16):
    loudness = block_scale(stream_key, dims, shards, -0.22, 0.18) if shards else 1.0
    drawn = jax.random.normal(stream_key, dims, jnp.float32) * scale * loudness
    return jnp.minimum(jnp.maximum(drawn, -reach), reach).astype(kind)


def setup_inputs(seed: int = 0) -> dict:
    keys = jax.random.split(jax.random.key(seed), 7)
    return {
        "d_proj": centred(keys[0], (GROUPS, GROUP_B, TABLES, P_SIZE), 1.0, 6.0, ((0, 96), (1, 8))),
        "pooled": centred(keys[1], (GROUPS, GROUP_B, TABLES, EMAX), 1.0, 6.0, ((0, 96), (1, 8))),
        "proj": centred(keys[2], (TABLES, EMAX, P_SIZE), EMAX ** -0.5, 0.25),
        "bag_rows": plant(ranked(keys[3], (GROUPS, GROUP_B, TABLES, BAG), ROWS, 2), jax.random.fold_in(keys[3], 3), 0, ROWS - 1).astype(jnp.int32),
        "bag_lengths": plant(jax.random.randint(keys[4], (GROUPS, GROUP_B, TABLES), 1, BAG + 1), jax.random.fold_in(keys[4], 1), 1, BAG).astype(jnp.int32),
        "dim_blocks": plant(jax.random.randint(keys[5], (TABLES,), 1, 17), jax.random.fold_in(keys[5], 1), 1, 16).astype(jnp.int32),
    }


def reference(d_proj, pooled, proj, bag_rows, bag_lengths, dim_blocks):
    columns = jnp.arange(EMAX, dtype=jnp.int32)
    live = (columns[None, :] < (UNIT * dim_blocks)[:, None]).astype(jnp.float32)
    row_ids = jnp.arange(ROWS, dtype=jnp.int32)

    def one_table(table):
        mask = live[table]
        weight = proj[table]

        def one_group(carry, group):
            dp = d_proj[group, :, table, :]
            pl = pooled[group, :, table, :]
            dpool = (jnp.dot(dp, weight.T, preferred_element_type=jnp.float32) * mask[None, :]).astype(jnp.bfloat16)
            plm = jnp.where(mask[None, :] > 0, pl, jnp.zeros_like(pl))
            pgrad = jnp.dot(plm.T, dp, preferred_element_type=jnp.float32)
            counts = jnp.zeros((GROUP_B, ROWS), jnp.float32)
            for slot in range(BAG):
                hit = (bag_rows[group, :, table, slot][:, None] == row_ids[None, :]) & (slot < bag_lengths[group, :, table])[:, None]
                counts = counts + hit.astype(jnp.float32)
            egrad = jnp.dot(counts.astype(jnp.bfloat16).T, dpool, preferred_element_type=jnp.float32)
            return (carry[0] + egrad, carry[1] + pgrad), None

        init = (jnp.zeros((ROWS, EMAX), jnp.float32), jnp.zeros((EMAX, P_SIZE), jnp.float32))
        result, _ = lax.scan(one_group, init, jnp.arange(GROUPS, dtype=jnp.int32))
        return result

    emb_grad, proj_grad = lax.map(one_table, jnp.arange(TABLES, dtype=jnp.int32))
    return emb_grad, proj_grad
```

```python
import jax
import jax.numpy as jnp
from jax import lax
from jax.sharding import PartitionSpec as P

ROWS = 512
LANES = 128
SUBLANES = 8
WIRE = jnp.float16


def stack_halves(part):
    return [part[:, at : at + LANES] for at in range(0, part.shape[1], LANES)]


def body(d_proj, pooled, proj, bag_rows, bag_lengths, dim_blocks):
    tables, widest, width = proj.shape
    group_rows = bag_rows.shape[1]
    bag_size = bag_rows.shape[3]
    peers = lax.axis_size("rep")
    table = lax.axis_index("tab")

    samples = lax.all_to_all(jnp.swapaxes(d_proj[0], 0, 1), "tab", 0, 0, tiled=True)
    samples = samples.reshape(group_rows, width)
    pools = lax.all_to_all(jnp.swapaxes(pooled[0], 0, 1), "tab", 0, 0, tiled=True)
    pools = pools.reshape(group_rows, widest)

    row_ids = jnp.arange(ROWS, dtype=jnp.int32)
    counts = jnp.zeros((ROWS, group_rows), jnp.float32)
    for slot in range(bag_size):
        hit = (bag_rows[0, :, 0, slot][None, :] == row_ids[:, None]) & (
            slot < bag_lengths[0, :, 0]
        )[None, :]
        counts = counts + hit.astype(jnp.float32)
    row_sums = jnp.dot(counts.astype(jnp.bfloat16), samples, preferred_element_type=jnp.float32)
    outer = lax.dot_general(
        pools, samples, (((0,), (0,)), ((), ())), preferred_element_type=jnp.float32
    )

    pieces = stack_halves(row_sums) + stack_halves(outer)
    rows = sum(piece.shape[0] for piece in pieces)
    share = -(-rows // (peers * SUBLANES)) * SUBLANES
    pad = jnp.zeros((share * peers - rows, LANES), WIRE)
    flat = jnp.concatenate([piece.astype(WIRE) for piece in pieces] + [pad], axis=0)
    parts = lax.all_to_all(flat.reshape(peers, share, LANES), "rep", 0, 0, tiled=True)
    total = jnp.sum(parts.astype(jnp.float32), axis=0)

    mine = jnp.broadcast_to((total * (1.0 / 128.0)).astype(WIRE)[None], (peers, share, LANES))
    full = lax.all_to_all(mine, "rep", 0, 0, tiled=True).reshape(peers * share, LANES)
    full = full.astype(jnp.float32) * 128.0
    half = width // LANES
    row_total = jnp.concatenate([full[i * ROWS : (i + 1) * ROWS] for i in range(half)], axis=1)
    base = half * ROWS
    proj_grad = jnp.concatenate(
        [full[base + i * widest : base + (i + 1) * widest] for i in range(half)], axis=1
    )

    limit = widest // 16 * lax.dynamic_index_in_dim(dim_blocks, table, 0, keepdims=False)
    live = jnp.arange(widest, dtype=jnp.int32) < limit
    weight = lax.dynamic_index_in_dim(proj, table, 0, keepdims=False)
    weight = jnp.where(live[:, None], weight, jnp.zeros_like(weight))
    high = row_total.astype(jnp.bfloat16)
    low = (row_total - high.astype(jnp.float32)).astype(jnp.bfloat16)
    emb_grad = lax.dot_general(
        high, weight, (((1,), (1,)), ((), ())), preferred_element_type=jnp.float32
    ) + lax.dot_general(low, weight, (((1,), (1,)), ((), ())), preferred_element_type=jnp.float32)
    proj_grad = jnp.where(live[:, None], proj_grad, 0.0)
    return (emb_grad[None], proj_grad[None])


def solution(mesh):
    placed = (
        P("rep", "tab", None, None),
        P("rep", "tab", None, None),
        P(),
        P("rep", None, "tab", None),
        P("rep", None, "tab"),
        P(),
    )
    return jax.shard_map(
        body,
        mesh=mesh,
        in_specs=placed,
        out_specs=(P("tab", None, None), P("tab", None, None)),
        check_vma=False,
    )
```

```python
import jax
import jax.numpy as jnp
from jax import lax
from jax.sharding import Mesh, PartitionSpec as P

ROWS = 512
LANES = 128
WIRE = jnp.float16
NEAR = ("zl", "y")
FAR = "zh"
REP = ("zh", "zl", "y")
Y = 8
ZL = 4


def halves(part):
    return [part[:, at : at + LANES] for at in range(0, part.shape[1], LANES)]


def to_all(block, axes, peers):
    return lax.all_to_all(
        jnp.broadcast_to(block[None], (peers,) + block.shape), axes, 0, 0, tiled=True
    )


def body(d_proj, pooled, proj, bag_rows, bag_lengths, dim_blocks):
    tables, widest, width = proj.shape
    group_rows = bag_rows.shape[1]
    bag_size = bag_rows.shape[3]
    near = lax.axis_size(NEAR)
    far = lax.axis_size(FAR)
    table = lax.axis_index("tab")

    both = jnp.concatenate(
        [jnp.swapaxes(d_proj[0], 0, 1), jnp.swapaxes(pooled[0], 0, 1)], axis=2
    )
    got = lax.all_to_all(both, "tab", 0, 0, tiled=True).reshape(group_rows, width + widest)
    samples, pools = got[:, :width], got[:, width:]

    row_ids = jnp.arange(ROWS, dtype=jnp.int32)
    counts = jnp.zeros((ROWS, group_rows), jnp.float32)
    for slot in range(bag_size):
        hit = (bag_rows[0, :, 0, slot][None, :] == row_ids[:, None]) & (
            slot < bag_lengths[0, :, 0]
        )[None, :]
        counts = counts + hit.astype(jnp.float32)
    limit = widest // 16 * lax.dynamic_index_in_dim(dim_blocks, table, 0, keepdims=False)
    live = jnp.arange(widest, dtype=jnp.int32) < limit
    weight = lax.dynamic_index_in_dim(proj, table, 0, keepdims=False)
    weight = jnp.where(live[:, None], weight, jnp.zeros_like(weight))
    counts, weight = lax.optimization_barrier(
        (counts.astype(jnp.bfloat16), jnp.concatenate([weight, weight], axis=1))
    )

    row_sums = jnp.dot(counts, samples, preferred_element_type=jnp.float32)
    outer = lax.dot_general(
        pools, samples, (((0,), (0,)), ((), ())), preferred_element_type=jnp.float32
    )

    flat = jnp.concatenate([piece.astype(WIRE) for piece in halves(row_sums) + halves(outer)], axis=0)
    parts = lax.all_to_all(flat.reshape(near, -1, LANES), NEAR, 0, 0, tiled=True)
    part = jnp.sum(parts.astype(jnp.float32), axis=0)
    part = to_all((part * (1.0 / 32.0)).astype(WIRE), FAR, far)
    total = jnp.sum(part.astype(jnp.float32), axis=0) * (32.0 / 128.0)
    full = to_all(total.astype(WIRE), NEAR, near).reshape(-1, LANES).astype(jnp.float32) * 128.0

    split = width // LANES
    row_total = jnp.concatenate([full[i * ROWS : (i + 1) * ROWS] for i in range(split)], axis=1)
    base = split * ROWS
    proj_grad = jnp.concatenate(
        [full[base + i * widest : base + (i + 1) * widest] for i in range(split)], axis=1
    )
    high = lax.reduce_precision(row_total, 8, 7)
    terms = jnp.concatenate([high, row_total - high], axis=1).astype(jnp.bfloat16)
    emb_grad = lax.dot_general(
        terms, weight, (((1,), (1,)), ((), ())), preferred_element_type=jnp.float32
    )
    proj_grad = jnp.where(live[:, None], proj_grad, 0.0)
    return (emb_grad[None], proj_grad[None])


def solution(mesh):
    tab = mesh.devices.shape[0]
    fine = Mesh(mesh.devices.reshape(tab, -1, ZL, Y), ("tab",) + REP)
    placed = (
        P(REP, "tab", None, None),
        P(REP, "tab", None, None),
        P(),
        P(REP, None, "tab", None),
        P(REP, None, "tab"),
        P(),
    )
    return jax.shard_map(
        body,
        mesh=fine,
        in_specs=placed,
        out_specs=(P("tab", None, None), P("tab", None, None)),
        check_vma=False,
    )
```

```python
import jax
import jax.numpy as jnp
from jax import lax
from jax.sharding import Mesh, PartitionSpec as P

ROWS = 512
LANES = 128
WIRE = jnp.float16
NEAR = ("y", "zl")
FAR = "zh"
REP = ("zh", "zl", "y")
Y = 8
ZL = 4


def halves(part):
    return [part[:, at : at + LANES] for at in range(0, part.shape[1], LANES)]


def to_all(block, axes, peers):
    return lax.all_to_all(
        jnp.broadcast_to(block[None], (peers,) + block.shape), axes, 0, 0, tiled=True
    )


def body(d_proj, pooled, proj, bag_rows, bag_lengths, dim_blocks):
    tables, widest, width = proj.shape
    group_rows = bag_rows.shape[1]
    bag_size = bag_rows.shape[3]
    near = lax.axis_size(NEAR)
    far = lax.axis_size(FAR)
    table = lax.axis_index("tab")

    both = jnp.concatenate(
        [jnp.swapaxes(d_proj[0], 0, 1), jnp.swapaxes(pooled[0], 0, 1)], axis=2
    )
    got = lax.all_to_all(both, "tab", 0, 0, tiled=True).reshape(group_rows, width + widest)
    samples, pools = got[:, :width], got[:, width:]

    row_ids = jnp.arange(ROWS, dtype=jnp.int32)
    counts = jnp.zeros((ROWS, group_rows), jnp.float32)
    for slot in range(bag_size):
        hit = (bag_rows[0, :, 0, slot][None, :] == row_ids[:, None]) & (
            slot < bag_lengths[0, :, 0]
        )[None, :]
        counts = counts + hit.astype(jnp.float32)
    limit = widest // 16 * lax.dynamic_index_in_dim(dim_blocks, table, 0, keepdims=False)
    live = jnp.arange(widest, dtype=jnp.int32) < limit
    weight = lax.dynamic_index_in_dim(proj, table, 0, keepdims=False)
    weight = jnp.where(live[:, None], weight, jnp.zeros_like(weight))
    counts, weight = lax.optimization_barrier(
        (counts.astype(jnp.bfloat16), jnp.concatenate([weight, weight], axis=1))
    )

    row_sums = jnp.dot(counts, samples, preferred_element_type=jnp.float32)
    outer = lax.dot_general(
        pools, samples, (((0,), (0,)), ((), ())), preferred_element_type=jnp.float32
    )

    flat = jnp.concatenate([piece.astype(WIRE) for piece in halves(row_sums) + halves(outer)], axis=0)
    parts = lax.all_to_all(flat.reshape(near, -1, LANES), NEAR, 0, 0, tiled=True)
    part = jnp.sum(parts.astype(jnp.float32), axis=0)
    mine = (part * (1.0 / 32.0)).astype(WIRE)
    seat = lax.axis_index(FAR)
    seats = [mine] + [
        lax.ppermute(mine, FAR, [(i, (i + hop) % far) for i in range(far)]) for hop in range(1, far)
    ]
    total = jnp.zeros(mine.shape, jnp.float32)
    for source in range(far):
        term = mine
        for hop in range(1, far):
            term = jnp.where((seat - hop) % far == source, seats[hop], term)
        total = total + term.astype(jnp.float32)
    total = total * (32.0 / 128.0)
    full = to_all(total.astype(WIRE), NEAR, near).reshape(-1, LANES).astype(jnp.float32) * 128.0

    split = width // LANES
    row_total = jnp.concatenate([full[i * ROWS : (i + 1) * ROWS] for i in range(split)], axis=1)
    base = split * ROWS
    proj_grad = jnp.concatenate(
        [full[base + i * widest : base + (i + 1) * widest] for i in range(split)], axis=1
    )
    high = lax.reduce_precision(row_total, 8, 7)
    terms = jnp.concatenate([high, row_total - high], axis=1).astype(jnp.bfloat16)
    emb_grad = lax.dot_general(
        terms, weight, (((1,), (1,)), ((), ())), preferred_element_type=jnp.float32
    )
    proj_grad = jnp.where(live[:, None], proj_grad, 0.0)
    return (emb_grad[None], proj_grad[None])


def solution(mesh):
    tab = mesh.devices.shape[0]
    fine = Mesh(mesh.devices.reshape(tab, -1, ZL, Y), ("tab",) + REP)
    placed = (
        P(REP, "tab", None, None),
        P(REP, "tab", None, None),
        P(),
        P(REP, None, "tab", None),
        P(REP, None, "tab"),
        P(),
    )
    return jax.shard_map(
        body,
        mesh=fine,
        in_specs=placed,
        out_specs=(P("tab", None, None), P("tab", None, None)),
        check_vma=False,
    )
```

```python
import jax
import jax.numpy as jnp
from jax import lax
from jax.experimental import pallas as pl
from jax.experimental.pallas import tpu as pltpu
from jax.sharding import Mesh, PartitionSpec as P

ROWS = 512
LANES = 128
WIRE = jnp.float16
NEAR = ("y", "zl")
FAR = "zh"
REP = ("zh", "zl", "y")
Y = 8
BLOCK = 32
ZL = 4


def halves(part):
    return [part[:, at : at + LANES] for at in range(0, part.shape[1], LANES)]


def to_all(block, axes, peers):
    return lax.all_to_all(
        jnp.broadcast_to(block[None], (peers,) + block.shape), axes, 0, 0, tiled=True
    )


def by_table(d_proj, pooled):
    samples, tables, width = d_proj.shape
    widest = pooled.shape[2]
    rows = BLOCK * tables

    def kernel(d_ref, p_ref, out_ref):
        to = lax.broadcasted_iota(jnp.int32, (rows, rows), 0)
        source = lax.broadcasted_iota(jnp.int32, (rows, rows), 1)
        swap = (source == (to % BLOCK) * tables + to // BLOCK).astype(jnp.bfloat16)
        for block in range(samples // BLOCK):
            at = slice(block * BLOCK, (block + 1) * BLOCK)
            for ref, left in ((d_ref, 0), (p_ref, width)):
                wide = ref.shape[2]
                moved = jnp.dot(
                    swap, ref[at].reshape(rows, wide), preferred_element_type=jnp.float32
                )
                out_ref[:, at, left : left + wide] = moved.astype(out_ref.dtype).reshape(
                    tables, BLOCK, wide
                )

    return pl.pallas_call(
        kernel,
        in_specs=[pl.BlockSpec(memory_space=pltpu.VMEM)] * 2,
        out_specs=pl.BlockSpec(memory_space=pltpu.VMEM),
        out_shape=jax.ShapeDtypeStruct((tables, samples, width + widest), d_proj.dtype),
        compiler_params=pltpu.CompilerParams(vmem_limit_bytes=60 * 2**20),
        cost_estimate=pl.CostEstimate(
            flops=2 * samples * tables * rows * (width + widest),
            transcendentals=0,
            bytes_accessed=4 * samples * tables * (width + widest),
        ),
    )(d_proj, pooled)


def finish(full, weight, limit):
    quarters, rows, lanes = full.shape
    widest, width = weight.shape
    tile = 256

    def kernel(limit_ref, full_ref, weight_ref, emb_ref, proj_ref):
        sums = full_ref[...] * 128.0
        row_total = jnp.concatenate([sums[0], sums[1]], axis=1)
        high = row_total.astype(jnp.bfloat16)
        low = (row_total - high.astype(jnp.float32)).astype(jnp.bfloat16)
        last = (((1,), (1,)), ((), ()))
        emb_ref[0] = lax.dot_general(
            high, weight_ref[...], last, preferred_element_type=jnp.float32
        ) + lax.dot_general(low, weight_ref[...], last, preferred_element_type=jnp.float32)
        row = lax.broadcasted_iota(jnp.int32, (tile, 1), 0) + pl.program_id(0) * tile
        proj_ref[0] = jnp.where(
            row < limit_ref[0], jnp.concatenate([sums[2], sums[3]], axis=1), 0.0
        )

    return pl.pallas_call(
        kernel,
        grid=(rows // tile,),
        in_specs=[
            pl.BlockSpec(memory_space=pltpu.SMEM),
            pl.BlockSpec((quarters, tile, lanes), lambda i: (0, i, 0)),
            pl.BlockSpec((widest, width), lambda i: (0, 0)),
        ],
        out_specs=[
            pl.BlockSpec((1, tile, widest), lambda i: (0, i, 0)),
            pl.BlockSpec((1, tile, width), lambda i: (0, i, 0)),
        ],
        out_shape=[
            jax.ShapeDtypeStruct((1, rows, widest), jnp.float32),
            jax.ShapeDtypeStruct((1, widest, width), jnp.float32),
        ],
        compiler_params=pltpu.CompilerParams(vmem_limit_bytes=16 * 2**20),
        cost_estimate=pl.CostEstimate(
            flops=4 * rows * widest * width, transcendentals=0, bytes_accessed=8 * rows * widest
        ),
    )(limit[None], full, weight)


def body(d_proj, pooled, proj, bag_rows, bag_lengths, dim_blocks):
    tables, widest, width = proj.shape
    group_rows = bag_rows.shape[1]
    bag_size = bag_rows.shape[3]
    near = lax.axis_size(NEAR)
    far = lax.axis_size(FAR)
    table = lax.axis_index("tab")

    got = lax.all_to_all(by_table(d_proj[0], pooled[0]), "tab", 0, 0, tiled=True).reshape(group_rows, width + widest)
    samples, pools = got[:, :width], got[:, width:]

    row_ids = jnp.arange(ROWS, dtype=jnp.int32)
    counts = jnp.zeros((ROWS, group_rows), jnp.float32)
    for slot in range(bag_size):
        hit = (bag_rows[0, :, 0, slot][None, :] == row_ids[:, None]) & (
            slot < bag_lengths[0, :, 0]
        )[None, :]
        counts = counts + hit.astype(jnp.float32)
    limit = widest // 16 * lax.dynamic_index_in_dim(dim_blocks, table, 0, keepdims=False)
    live = jnp.arange(widest, dtype=jnp.int32) < limit
    weight = lax.dynamic_index_in_dim(proj, table, 0, keepdims=False)
    weight = jnp.where(live[:, None], weight, jnp.zeros_like(weight))
    counts, weight = lax.optimization_barrier((counts.astype(jnp.bfloat16), weight))

    row_sums = jnp.dot(counts, samples, preferred_element_type=jnp.float32)
    outer = lax.dot_general(
        pools, samples, (((0,), (0,)), ((), ())), preferred_element_type=jnp.float32
    )

    flat = jnp.concatenate([piece.astype(WIRE) for piece in halves(row_sums) + halves(outer)], axis=0)
    parts = lax.all_to_all(flat.reshape(near, -1, LANES), NEAR, 0, 0, tiled=True)
    part = jnp.sum(parts.astype(jnp.float32), axis=0)
    part = to_all((part * (1.0 / 32.0)).astype(WIRE), FAR, far)
    total = jnp.sum(part.astype(jnp.float32), axis=0) * (32.0 / 128.0)
    full = to_all(total.astype(WIRE), NEAR, near).astype(jnp.float32)
    emb_grad, proj_grad = finish(full.reshape(-1, ROWS, LANES), weight, limit)
    return (emb_grad, proj_grad)


def solution(mesh):
    tab = mesh.devices.shape[0]
    fine = Mesh(mesh.devices.reshape(tab, -1, ZL, Y), ("tab",) + REP)
    placed = (
        P(REP, "tab", None, None),
        P(REP, "tab", None, None),
        P(),
        P(REP, None, "tab", None),
        P(REP, None, "tab"),
        P(),
    )
    return jax.shard_map(
        body,
        mesh=fine,
        in_specs=placed,
        out_specs=(P("tab", None, None), P("tab", None, None)),
        check_vma=False,
    )
```

```python
import jax
import jax.numpy as jnp
from jax import lax
from jax.experimental import pallas as pl
from jax.experimental.pallas import tpu as pltpu
from jax.sharding import Mesh, PartitionSpec as P

ROWS = 512
WIRE = jnp.float16
NEAR = ("y", "zl")
FAR = "zh"
REP = ("zh", "zl", "y")
Y = 8
BLOCK = 32
ZL = 4


def to_all(block, axes, peers):
    return lax.all_to_all(
        jnp.broadcast_to(block[None], (peers,) + block.shape), axes, 0, 0, tiled=True
    )


def by_table(d_proj, pooled):
    samples, tables, width = d_proj.shape
    widest = pooled.shape[2]
    rows = BLOCK * tables

    step = BLOCK * 2

    def kernel(d_ref, p_ref, out_ref):
        to = lax.broadcasted_iota(jnp.int32, (rows, rows), 0)
        source = lax.broadcasted_iota(jnp.int32, (rows, rows), 1)
        swap = (source == (to % BLOCK) * tables + to // BLOCK).astype(jnp.bfloat16)
        for block in range(step // BLOCK):
            at = slice(block * BLOCK, (block + 1) * BLOCK)
            for ref, left in ((d_ref, 0), (p_ref, width)):
                wide = ref.shape[2]
                moved = jnp.dot(
                    swap, ref[at].reshape(rows, wide), preferred_element_type=jnp.float32
                )
                out_ref[:, at, left : left + wide] = moved.astype(out_ref.dtype).reshape(
                    tables, BLOCK, wide
                )

    return pl.pallas_call(
        kernel,
        grid=(samples // step,),
        in_specs=[
            pl.BlockSpec((step, tables, width), lambda i: (i, 0, 0)),
            pl.BlockSpec((step, tables, widest), lambda i: (i, 0, 0)),
        ],
        out_specs=pl.BlockSpec((tables, step, width + widest), lambda i: (0, i, 0)),
        out_shape=jax.ShapeDtypeStruct((tables, samples, width + widest), d_proj.dtype),
        compiler_params=pltpu.CompilerParams(vmem_limit_bytes=60 * 2**20),
        cost_estimate=pl.CostEstimate(
            flops=2 * samples * tables * rows * (width + widest),
            transcendentals=0,
            bytes_accessed=4 * samples * tables * (width + widest),
        ),
    )(d_proj, pooled)


def finish(full, weight, limit):
    kinds, rows, width = full.shape
    widest = weight.shape[0]
    tile = 256

    def kernel(limit_ref, full_ref, weight_ref, emb_ref, proj_ref):
        sums = full_ref[...] * 128.0
        row_total = sums[0]
        high = row_total.astype(jnp.bfloat16)
        low = (row_total - high.astype(jnp.float32)).astype(jnp.bfloat16)
        last = (((1,), (1,)), ((), ()))
        emb_ref[0] = lax.dot_general(
            high, weight_ref[...], last, preferred_element_type=jnp.float32
        ) + lax.dot_general(low, weight_ref[...], last, preferred_element_type=jnp.float32)
        row = lax.broadcasted_iota(jnp.int32, (tile, 1), 0) + pl.program_id(0) * tile
        proj_ref[0] = jnp.where(row < limit_ref[0], sums[1], 0.0)

    return pl.pallas_call(
        kernel,
        grid=(rows // tile,),
        in_specs=[
            pl.BlockSpec(memory_space=pltpu.SMEM),
            pl.BlockSpec((kinds, tile, width), lambda i: (0, i, 0)),
            pl.BlockSpec((widest, width), lambda i: (0, 0)),
        ],
        out_specs=[
            pl.BlockSpec((1, tile, widest), lambda i: (0, i, 0)),
            pl.BlockSpec((1, tile, width), lambda i: (0, i, 0)),
        ],
        out_shape=[
            jax.ShapeDtypeStruct((1, rows, widest), jnp.float32),
            jax.ShapeDtypeStruct((1, widest, width), jnp.float32),
        ],
        compiler_params=pltpu.CompilerParams(vmem_limit_bytes=16 * 2**20),
        cost_estimate=pl.CostEstimate(
            flops=4 * rows * widest * width, transcendentals=0, bytes_accessed=8 * rows * widest
        ),
    )(limit[None], full, weight)


def body(d_proj, pooled, proj, bag_rows, bag_lengths, dim_blocks):
    tables, widest, width = proj.shape
    group_rows = bag_rows.shape[1]
    bag_size = bag_rows.shape[3]
    near = lax.axis_size(NEAR)
    far = lax.axis_size(FAR)
    table = lax.axis_index("tab")

    got = lax.all_to_all(by_table(d_proj[0], pooled[0]), "tab", 0, 0, tiled=True).reshape(group_rows, width + widest)
    samples, pools = got[:, :width], got[:, width:]

    row_ids = jnp.arange(ROWS, dtype=jnp.int32)
    counts = jnp.zeros((ROWS, group_rows), jnp.float32)
    for slot in range(bag_size):
        hit = (bag_rows[0, :, 0, slot][None, :] == row_ids[:, None]) & (
            slot < bag_lengths[0, :, 0]
        )[None, :]
        counts = counts + hit.astype(jnp.float32)
    limit = widest // 16 * lax.dynamic_index_in_dim(dim_blocks, table, 0, keepdims=False)
    live = jnp.arange(widest, dtype=jnp.int32) < limit
    weight = lax.dynamic_index_in_dim(proj, table, 0, keepdims=False)
    weight = jnp.where(live[:, None], weight, jnp.zeros_like(weight))
    counts, weight = lax.optimization_barrier((counts.astype(jnp.bfloat16), weight))

    row_sums = jnp.dot(counts, samples, preferred_element_type=jnp.float32)
    outer = lax.dot_general(
        pools, samples, (((0,), (0,)), ((), ())), preferred_element_type=jnp.float32
    )

    flat = jnp.concatenate([row_sums.astype(WIRE), outer.astype(WIRE)], axis=0)
    parts = lax.all_to_all(flat.reshape(near, -1, width), NEAR, 0, 0, tiled=True)
    part = jnp.sum(parts.astype(jnp.float32), axis=0)
    part = to_all((part * (1.0 / 32.0)).astype(WIRE), FAR, far)
    total = jnp.sum(part.astype(jnp.float32), axis=0) * (32.0 / 128.0)
    full = to_all(total.astype(WIRE), NEAR, near).astype(jnp.float32)
    emb_grad, proj_grad = finish(full.reshape(2, ROWS, width), weight, limit)
    return (emb_grad, proj_grad)


def solution(mesh):
    tab = mesh.devices.shape[0]
    fine = Mesh(mesh.devices.reshape(tab, -1, ZL, Y), ("tab",) + REP)
    placed = (
        P(REP, "tab", None, None),
        P(REP, "tab", None, None),
        P(),
        P(REP, None, "tab", None),
        P(REP, None, "tab"),
        P(),
    )
    return jax.shard_map(
        body,
        mesh=fine,
        in_specs=placed,
        out_specs=(P("tab", None, None), P("tab", None, None)),
        check_vma=False,
    )
```

```python
import jax
import jax.numpy as jnp
from jax import lax
from jax.experimental import pallas as pl
from jax.experimental.pallas import tpu as pltpu
from jax.sharding import Mesh, PartitionSpec as P

ROWS = 512
WIRE = jnp.float16
NEAR = ("y", "zl")
FAR = "zh"
REP = ("zh", "zl", "y")
Y = 8
BLOCK = 32
ZL = 4


def to_all(block, axes, peers):
    return lax.all_to_all(
        jnp.broadcast_to(block[None], (peers,) + block.shape), axes, 0, 0, tiled=True
    )


def by_table(d_proj, pooled):
    samples, tables, width = d_proj.shape
    widest = pooled.shape[2]
    rows = BLOCK * tables

    step = BLOCK * 2

    def kernel(d_ref, p_ref, out_ref):
        to = lax.broadcasted_iota(jnp.int32, (rows, rows), 0)
        source = lax.broadcasted_iota(jnp.int32, (rows, rows), 1)
        sample, table = to & (BLOCK - 1), lax.shift_right_logical(to, BLOCK.bit_length() - 1)
        swap = (source == sample * tables + table).astype(jnp.bfloat16)
        for block in range(step // BLOCK):
            at = slice(block * BLOCK, (block + 1) * BLOCK)
            for ref, left in ((d_ref, 0), (p_ref, width)):
                wide = ref.shape[2]
                moved = jnp.dot(
                    swap, ref[at].reshape(rows, wide), preferred_element_type=jnp.float32
                )
                out_ref[:, at, left : left + wide] = moved.astype(out_ref.dtype).reshape(
                    tables, BLOCK, wide
                )

    return pl.pallas_call(
        kernel,
        grid=(samples // step,),
        in_specs=[
            pl.BlockSpec((step, tables, width), lambda i: (i, 0, 0)),
            pl.BlockSpec((step, tables, widest), lambda i: (i, 0, 0)),
        ],
        out_specs=pl.BlockSpec((tables, step, width + widest), lambda i: (0, i, 0)),
        out_shape=jax.ShapeDtypeStruct((tables, samples, width + widest), d_proj.dtype),
        compiler_params=pltpu.CompilerParams(vmem_limit_bytes=60 * 2**20),
        cost_estimate=pl.CostEstimate(
            flops=2 * samples * tables * rows * (width + widest),
            transcendentals=0,
            bytes_accessed=4 * samples * tables * (width + widest),
        ),
    )(d_proj, pooled)


def finish(full, weight, limit):
    kinds, rows, width = full.shape
    widest = weight.shape[0]
    tile = 256

    def kernel(limit_ref, full_ref, weight_ref, emb_ref, proj_ref):
        sums = full_ref[...] * 128.0
        row_total = sums[0]
        high = row_total.astype(jnp.bfloat16)
        low = (row_total - high.astype(jnp.float32)).astype(jnp.bfloat16)
        last = (((1,), (1,)), ((), ()))
        emb_ref[0] = lax.dot_general(
            high, weight_ref[...], last, preferred_element_type=jnp.float32
        ) + lax.dot_general(low, weight_ref[...], last, preferred_element_type=jnp.float32)
        row = lax.broadcasted_iota(jnp.int32, (tile, 1), 0) + pl.program_id(0) * tile
        proj_ref[0] = jnp.where(row < limit_ref[0], sums[1], 0.0)

    return pl.pallas_call(
        kernel,
        grid=(rows // tile,),
        in_specs=[
            pl.BlockSpec(memory_space=pltpu.SMEM),
            pl.BlockSpec((kinds, tile, width), lambda i: (0, i, 0)),
            pl.BlockSpec((widest, width), lambda i: (0, 0)),
        ],
        out_specs=[
            pl.BlockSpec((1, tile, widest), lambda i: (0, i, 0)),
            pl.BlockSpec((1, tile, width), lambda i: (0, i, 0)),
        ],
        out_shape=[
            jax.ShapeDtypeStruct((1, rows, widest), jnp.float32),
            jax.ShapeDtypeStruct((1, widest, width), jnp.float32),
        ],
        compiler_params=pltpu.CompilerParams(vmem_limit_bytes=16 * 2**20),
        cost_estimate=pl.CostEstimate(
            flops=4 * rows * widest * width, transcendentals=0, bytes_accessed=8 * rows * widest
        ),
    )(limit[None], full, weight)


def body(d_proj, pooled, proj, bag_rows, bag_lengths, dim_blocks):
    tables, widest, width = proj.shape
    group_rows = bag_rows.shape[1]
    bag_size = bag_rows.shape[3]
    near = lax.axis_size(NEAR)
    far = lax.axis_size(FAR)
    table = lax.axis_index("tab")

    got = lax.all_to_all(by_table(d_proj[0], pooled[0]), "tab", 0, 0, tiled=True).reshape(group_rows, width + widest)
    samples, pools = got[:, :width], got[:, width:]

    row_ids = jnp.arange(ROWS, dtype=jnp.int32)
    counts = jnp.zeros((ROWS, group_rows), jnp.float32)
    for slot in range(bag_size):
        hit = (bag_rows[0, :, 0, slot][None, :] == row_ids[:, None]) & (
            slot < bag_lengths[0, :, 0]
        )[None, :]
        counts = counts + hit.astype(jnp.float32)
    limit = widest // 16 * lax.dynamic_index_in_dim(dim_blocks, table, 0, keepdims=False)
    live = jnp.arange(widest, dtype=jnp.int32) < limit
    weight = lax.dynamic_index_in_dim(proj, table, 0, keepdims=False)
    weight = jnp.where(live[:, None], weight, jnp.zeros_like(weight))
    counts, weight = lax.optimization_barrier((counts.astype(jnp.bfloat16), weight))

    row_sums = jnp.dot(counts, samples, preferred_element_type=jnp.float32)
    outer = lax.dot_general(
        pools, samples, (((0,), (0,)), ((), ())), preferred_element_type=jnp.float32
    )

    flat = jnp.concatenate([row_sums.astype(WIRE), outer.astype(WIRE)], axis=0)
    parts = lax.all_to_all(flat.reshape(near, -1, width), NEAR, 0, 0, tiled=True)
    part = jnp.sum(parts.astype(jnp.float32), axis=0)
    part = to_all((part * (1.0 / 32.0)).astype(WIRE), FAR, far)
    total = jnp.sum(part.astype(jnp.float32), axis=0) * (32.0 / 128.0)
    full = to_all(total.astype(WIRE), NEAR, near).astype(jnp.float32)
    emb_grad, proj_grad = finish(full.reshape(2, ROWS, width), weight, limit)
    return (emb_grad, proj_grad)


def solution(mesh):
    tab = mesh.devices.shape[0]
    fine = Mesh(mesh.devices.reshape(tab, -1, ZL, Y), ("tab",) + REP)
    placed = (
        P(REP, "tab", None, None),
        P(REP, "tab", None, None),
        P(),
        P(REP, None, "tab", None),
        P(REP, None, "tab"),
        P(),
    )
    return jax.shard_map(
        body,
        mesh=fine,
        in_specs=placed,
        out_specs=(P("tab", None, None), P("tab", None, None)),
        check_vma=False,
    )
```
